32 devices in a mesh: dp: 8 (over y, x, core), ctx: 4 (over z).
Axes of the slice: x: 2, y: 2, z: 4, core: 2. Of those that a mesh axis runs over, the one named last changes fastest.
Arguments:
- layer_input: bfloat16 [8, 512, 1024], P('dp', 'ctx'), may hold values from -6 to 6
- projected: bfloat16 [8, 512, 3072], P('dp', 'ctx'), may hold values from -6 to 6
- grad_output: bfloat16 [8, 512, 1024], P('dp', 'ctx'), may hold values from -12 to 12
- w_qkv: bfloat16 [1024, 3072], P('dp', 'ctx'), may hold values from -0.1875 to 0.1875
- lengths: int32 [8, 8], P('dp'), may hold values from 1 to 256, 512 in all within a row
- block_perm: int32 [8, 4], P('dp'), may hold values from 0 to 3, each once within a row
Outputs:
- grad_input: bfloat16 [8, 512, 1024], P('dp', 'ctx')
- grad_weight: float32 [1024, 3072], P('dp', 'ctx')
The draws below stay inside these ranges and needn't reach their ends.
Inputs may be any that keep to these rules, and one draw needn't show every extreme that they name: Every row of lengths sums to 512 and has an entry equal to 256. Every row of block_perm names each of the 4 blocks once; slot block s holds packed positions block_perm[g, s] * 128 to block_perm[g, s] * 128 + 127.
All inputs are finite; a program needn't handle non-finite values.
Results may differ from the reference program's by a relative error of at most 0.0065.
Values may be sent and summed in bfloat16 or wider, within the bound.
No kernel may reach another device: no remote copies, remote signals or barrier semaphores. Data moves between devices by JAX's collectives and lax.ppermute only.
A program may use at most 64 MiB of HBM per device.

```python
import math
import jax
import jax.numpy as jnp
import numpy as np
from jax import lax

D = 1024
HEADS = 16
DH = 64
BLK = 128
USERS = 8
CTX_TOK = 512
MAXLEN = 256
NBLK = 4
GROUPS = 8
N_CTX = 4


def spiked(array, stream_key, source, target, blocks, factor):
    owner, partner = [(jnp.arange(array.shape[dim]) // (array.shape[dim] // blocks)).reshape([-1 if axis == dim else 1 for axis in range(array.ndim)]) for dim in (source, target)]
    chosen = jax.random.permutation(stream_key, blocks)[partner]
    strong = (owner == chosen) | (owner == (partner + blocks // 2) % blocks)
    return jnp.where(strong, factor * array, array)


def block_levels(own_key, extent, cuts, low, largest):
    level, own = 1.0, jax.random.fold_in(own_key, 6)
    for axis_at, blocks in cuts:
        draws = jnp.exp(jax.random.uniform(jax.random.fold_in(own, axis_at), (blocks,), jnp.float32, low / len(cuts), largest / len(cuts)))
        level = level * jnp.repeat(draws, extent[axis_at] // blocks).reshape([-1 if axis == axis_at else 1 for axis in range(len(extent))])
    return level


def length_profile(count, total, limit, lean):
    portions = [(1 << 20) // math.isqrt(rank ** lean) + 1 for rank in range(2, count + 1)]
    surplus, counts = total - limit - (count - 1), [1] * (count - 1)
    while surplus > 0:
        free = [i for i in range(count - 1) if counts[i] < limit]
        pool, left = sum([portions[i] for i in free]), surplus
        for i in free:
            addition = min(limit - counts[i], max(1, left * portions[i] // pool), surplus)
            counts[i] = counts[i] + addition
            surplus = surplus - addition
    return np.array([limit] + counts)


def ragged_sizes(rng, count, total, bound, lean):
    if count == 2:
        one = jax.random.randint(rng, (), max(1, total - bound), min(bound, total - 1) + 1)
        return jnp.stack([one, total - one])
    sizes = jnp.asarray(length_profile(count, total, bound, lean), jnp.int32)
    twos = (count - 1) // 2
    giver, sink = sizes[1:1 + 2 * twos:2], sizes[2:2 + 2 * twos:2]
    margin = jnp.minimum(giver - 1, bound - sink)
    shifted = jax.random.randint(jax.random.fold_in(rng, 1), (twos,), 0, 1 << 20) % (margin + 1)
    sizes = sizes.at[1:1 + 2 * twos:2].set(giver - shifted).at[2:2 + 2 * twos:2].set(sink + shifted)
    return sizes[jax.random.permutation(jax.random.fold_in(rng, 2), count)]


def noise(own_key, shape, deviation, limit, split=(), kind=jnp.bfloat16):
    factor_of = block_levels(own_key, shape, split, -0.22, 0.18) if split else 1.0
    entries = jax.random.normal(own_key, shape, jnp.float32) * deviation * factor_of
    return jnp.minimum(jnp.maximum(entries, -limit), limit).astype(kind)


def bell_draw_with(key, shape, scale, limit, cuts, heavy, held_as=jnp.bfloat16):
    drawn = scale * jax.random.normal(key, shape, jnp.float32)
    if cuts:
        drawn = drawn * block_levels(key, shape, cuts, -0.22, 0.18)
    return jnp.clip(spiked(drawn, jax.random.fold_in(key, 3), *heavy), -limit, limit).astype(held_as)


def setup_inputs(seed: int = 0) -> dict:
    arg_keys = jax.random.split(jax.random.key(seed), 7)
    layer_input = bell_draw_with(arg_keys[0], (GROUPS, CTX_TOK, D), 1.0, 6.0, ((0, 8), (1, 4)), (0, 2, 8, 2.0))
    projected = noise(arg_keys[1], (GROUPS, CTX_TOK, 3 * D), 1.0, 6.0, ((0, 8), (1, 4)))
    grad_output = noise(arg_keys[2], (GROUPS, CTX_TOK, D), 2.0, 12.0, ((0, 8), (1, 4)))
    w_qkv = noise(arg_keys[3], (D, 3 * D), D ** -0.5, 0.1875, ((0, 8), (1, 4)))
    lengths = jax.vmap(lambda own: ragged_sizes(own, USERS, CTX_TOK, MAXLEN, 2))(jax.random.split(arg_keys[4], GROUPS)).reshape((GROUPS, USERS)).astype(jnp.int32)
    block_perm = jax.vmap(lambda own: jax.random.permutation(own, NBLK))(jax.random.split(arg_keys[5], GROUPS)).reshape((GROUPS, NBLK)).astype(jnp.int32)
    return {"layer_input": layer_input, "projected": projected, "grad_output": grad_output, "w_qkv": w_qkv, "lengths": lengths, "block_perm": block_perm}


def silu_slope(value):
    sigma = jax.nn.sigmoid(value)
    return sigma * (1.0 + value * (1.0 - sigma))

def row_layout(user_lengths, slot_blocks):
    slots = jnp.arange(CTX_TOK, dtype=jnp.int32)
    position = slot_blocks[slots // BLK] * BLK + slots % BLK
    ends = jnp.cumsum(user_lengths).astype(jnp.int32)
    segment = lax.optimization_barrier(jnp.sum((position[:, None] >= ends[None, :]).astype(jnp.int32), axis=1))
    member = segment[:, None] == jnp.arange(USERS, dtype=jnp.int32)[None, :]
    user_len = lax.optimization_barrier(jnp.sum(jnp.where(member, user_lengths[None, :], 0), axis=1))
    row_scale = lax.rsqrt(user_len.astype(jnp.float32))
    return (position, segment, row_scale)

def head_backward(pre_head, grad_head, position, segment, row_scale):
    active = jax.nn.silu(pre_head.astype(jnp.float32)).astype(jnp.bfloat16)
    queries = active[:, 0]
    key_rows = active[:, 1]
    value_rows = active[:, 2]
    scale = DH ** (-0.5)
    scores = jnp.dot(queries, key_rows.T, preferred_element_type=jnp.float32) * scale
    visible = (segment[:, None] == segment[None, :]) & (position[None, :] <= position[:, None])
    sigma = jax.nn.sigmoid(scores)
    weights = jnp.where(visible, scores * sigma * row_scale[:, None], 0.0).astype(jnp.bfloat16)
    grad_weights = jnp.dot(grad_head, value_rows.T, preferred_element_type=jnp.float32)
    slope = grad_weights * sigma * (1.0 + scores * (1.0 - sigma)) * (row_scale[:, None] * scale)
    grad_scores = jnp.where(visible, slope, 0.0).astype(jnp.bfloat16)
    grad_query = jnp.dot(grad_scores, key_rows, preferred_element_type=jnp.float32)
    grad_key = jnp.dot(grad_scores.T, queries, preferred_element_type=jnp.float32)
    grad_value = jnp.dot(weights.T, grad_head, preferred_element_type=jnp.float32)
    grads = jnp.stack([grad_query, grad_key, grad_value], axis=1)
    return (grads * silu_slope(pre_head.astype(jnp.float32))).astype(jnp.bfloat16)

def input_gradient(grad_pre, weight):
    group_cols = 3 * D // N_CTX
    pre_groups = grad_pre.reshape(CTX_TOK, N_CTX, group_cols).transpose(1, 0, 2)
    weight_groups = weight.reshape(D, N_CTX, group_cols).transpose(1, 0, 2)

    def add_group(total, item):
        term = jnp.dot(item[0], item[1].T, preferred_element_type=jnp.float32).astype(jnp.bfloat16)
        return (total + lax.optimization_barrier(term).astype(jnp.float32), None)
    total, unused = lax.scan(add_group, jnp.zeros((CTX_TOK, D), jnp.float32), (pre_groups, weight_groups))
    return total.astype(jnp.bfloat16)

def reference(layer_input, projected, grad_output, w_qkv, lengths, block_perm):

    def one_group(weight_total, group_item):
        tokens, pre_group, grad_group, user_lengths, slot_blocks = group_item
        position, segment, row_scale = row_layout(user_lengths, slot_blocks)
        pre_heads = pre_group.reshape(CTX_TOK, HEADS, 3, DH).transpose(1, 0, 2, 3)
        grad_heads = grad_group.reshape(CTX_TOK, HEADS, DH).transpose(1, 0, 2)

        def per_head(operands):
            return head_backward(operands[0], operands[1], position, segment, row_scale)
        head_grads = lax.map(per_head, (pre_heads, grad_heads))
        grad_pre = head_grads.transpose(1, 0, 2, 3).reshape(CTX_TOK, 3 * D)
        grad_rows = input_gradient(grad_pre, w_qkv)
        weight_total = weight_total + jnp.dot(tokens.T, grad_pre, preferred_element_type=jnp.float32)
        return (weight_total, grad_rows)
    weight_total, grad_input = lax.scan(one_group, jnp.zeros((D, 3 * D), jnp.float32), (layer_input, projected, grad_output, lengths, block_perm))
    return (grad_input, weight_total * (1.0 / GROUPS))
```

```python
import jax
import jax.numpy as jnp
from jax import lax
from jax.experimental import pallas as pl
from jax.experimental.pallas import tpu as pltpu
from jax.sharding import PartitionSpec as P

DH = 64
VMEM_BYTES = 48 * 1024 * 1024
BY_ROWS = (((0,), (0,)), ((), ()))
BY_COLS = (((1,), (1,)), ((), ()))


def dot(a, b, dims):
    return lax.dot_general(a, b, dims, preferred_element_type=jnp.float32)


def in_vmem():
    return pl.BlockSpec(memory_space=pltpu.VMEM)


def in_smem():
    return pl.BlockSpec(memory_space=pltpu.SMEM)


def call(kernel, scalars, arrays, outs, scratch=(), flops=0):
    size = sum(a.size * a.dtype.itemsize for a in arrays) + sum(
        o.size * o.dtype.itemsize for o in outs
    )
    return pl.pallas_call(
        kernel,
        out_shape=list(outs),
        in_specs=[in_smem()] * len(scalars) + [in_vmem()] * len(arrays),
        out_specs=[in_vmem()] * len(outs),
        scratch_shapes=list(scratch),
        compiler_params=pltpu.CompilerParams(vmem_limit_bytes=VMEM_BYTES),
        cost_estimate=pl.CostEstimate(flops=flops, bytes_accessed=size, transcendentals=0),
    )(*scalars, *arrays)


def bf16(*shape):
    return jax.ShapeDtypeStruct(shape, jnp.bfloat16)


def f32(*shape):
    return jax.ShapeDtypeStruct(shape, jnp.float32)


def swap(array, axis, mask):
    count = lax.axis_size(axis)
    return lax.ppermute(array, axis, [(i, i ^ mask) for i in range(count)])


def gather(array, axis):
    held, mask = {0: array}, lax.axis_size(axis) // 2
    while mask:
        for near in sorted(held):
            held[near ^ mask] = swap(held[near], axis, mask)
        mask //= 2
    return [held[r] for r in sorted(held)]


def pack(ctx_index, pre, grad, ctx_count, parts, heads):
    rows = pre.shape[0]
    wide, narrow = heads * 3 * DH, heads * DH
    if wide % 128 or narrow % 128:
        both = jnp.concatenate(
            [
                pre.reshape(rows, ctx_count, parts, wide),
                grad.reshape(rows, ctx_count, parts, narrow),
            ],
            axis=3,
        ).transpose(1, 2, 0, 3)
        owners = [lax.dynamic_index_in_dim(both, ctx_index ^ r, 0, False) for r in range(ctx_count)]
        return [[owner[part] for owner in owners] for part in range(parts)]

    def kernel(me_ref, pre_ref, grad_ref, *out_refs):
        for part in range(parts):
            for r in range(ctx_count):
                owner = (me_ref[0] ^ r) * parts + part
                out = out_refs[part * ctx_count + r]
                out[:, :wide] = pre_ref[:, pl.ds(pl.multiple_of(owner * wide, 128), wide)]
                out[:, wide:] = grad_ref[:, pl.ds(pl.multiple_of(owner * narrow, 128), narrow)]

    outs = call(
        kernel,
        [ctx_index[None]],
        [pre, grad],
        [bf16(rows, wide + narrow)] * (parts * ctx_count),
    )
    return [outs[part * ctx_count : (part + 1) * ctx_count] for part in range(parts)]


def head_grads(lengths_ref, act, pre, out_ref, heads, rows, blocks, column):
    whole = rows * blocks
    place = lax.broadcasted_iota(jnp.int32, (8, whole), 1)
    first = jnp.zeros((8, whole), jnp.int32)
    length = jnp.zeros((8, whole), jnp.int32)
    start = jnp.int32(0)
    for user in range(lengths_ref.shape[1]):
        inside = place >= start
        first = jnp.where(inside, start, first)
        length = jnp.where(inside, lengths_ref[0, user], length)
        start = start + lengths_ref[0, user]
    scale = lax.rsqrt(length.astype(jnp.float32))[:1]
    first = first[:1]
    grad_q = [[None] * blocks for _ in range(heads)]
    for j in range(blocks):
        lo = j * rows
        count = whole - lo
        key_place = lax.broadcasted_iota(jnp.int32, (rows, count), 0)
        query_place = lax.broadcasted_iota(jnp.int32, (rows, count), 1)
        visible = (query_place >= key_place) & (key_place + lo >= first[:, lo:])
        scales = jnp.where(visible, scale[:, lo:], 0.0)
        for h in range(heads):
            base = h * 3 * DH
            query = act[lo:, base : base + DH]
            key = act[lo : lo + rows, base + DH : base + 2 * DH]
            value = act[lo : lo + rows, base + 2 * DH : base + 3 * DH]
            grad = act[lo:, heads * 3 * DH + h * DH : heads * 3 * DH + (h + 1) * DH]
            u = dot(key, query, BY_COLS)
            gw = dot(value, grad, BY_COLS)
            t = jnp.tanh(u)
            a = scales + scales * t
            weights = (u * a).astype(jnp.bfloat16)
            slope = (gw * a * (1.0 + (u - u * t))).astype(jnp.bfloat16)
            grad_v = dot(weights, grad, (((1,), (0,)), ((), ())))
            grad_k = dot(slope, query, (((1,), (0,)), ((), ())))
            add_q = dot(slope, key, BY_ROWS)
            for i in range(j, blocks):
                term = add_q[(i - j) * rows : (i - j + 1) * rows]
                grad_q[h][i] = term if j == 0 else grad_q[h][i] + term
            for part, value_grad in ((1, grad_k), (2, grad_v), (0, grad_q[h][j])):
                at = base + part * DH
                z = pre[lo : lo + rows, at : at + DH].astype(jnp.float32)
                s = 0.5 + 0.5 * jnp.tanh(0.5 * z)
                factor = s * (1.0 + z * (1.0 - s))
                if part == 0:
                    factor = factor * 0.0625
                out_ref[lo : lo + rows, column + at : column + at + DH] = (
                    value_grad * factor
                ).astype(jnp.bfloat16)


def load_pieces(perm_ref, me, piece_refs, pre, act, heads, rows):
    wide = heads * 3 * DH
    for r, piece in enumerate(piece_refs):
        at = pl.ds(pl.multiple_of(perm_ref[0, me ^ r] * rows, rows), rows)
        value = piece[...]
        pre[at, :] = value[:, :wide]
        z = value[:, :wide].astype(jnp.float32)
        active = (z * (0.5 + 0.5 * jnp.tanh(0.5 * z))).astype(jnp.bfloat16)
        column = lax.broadcasted_iota(jnp.int32, active.shape, 1) % (3 * DH)
        act[at, :wide] = jnp.where(column < DH, active * jnp.bfloat16(0.0625), active)
        act[at, wide:] = value[:, wide:]


def body(layer_input, projected, grad_output, w_qkv, lengths, block_perm):
    rows, width = layer_input.shape[1:]
    ctx_count, dp_count = lax.axis_size("ctx"), lax.axis_size("dp")
    me_ctx, me_dp = lax.axis_index("ctx"), lax.axis_index("dp")
    whole = rows * ctx_count
    local_heads = width // DH // ctx_count
    parts = 2 if local_heads % 4 == 0 else 1
    heads = local_heads // parts
    wide = heads * 3 * DH
    columns = parts * wide
    w_rows = w_qkv.shape[0]
    part_flops = 10 * heads * whole * whole * DH
    product_flops = 2 * whole * columns * width

    pieces = pack(me_ctx, projected[0], grad_output[0], ctx_count, parts, heads)
    arrived = [
        [pieces[part][0]]
        + [swap(pieces[part][r], "ctx", r) for r in range(1, ctx_count)]
        for part in range(parts)
    ]
    weights = gather(w_qkv, "dp")
    tokens = gather(layer_input[0], "ctx")

    scratch = [
        pltpu.VMEM((whole, wide), jnp.bfloat16),
        pltpu.VMEM((whole, wide + heads * DH), jnp.bfloat16),
    ]

    def attention(lengths_ref, perm_ref, me_ref, *refs):
        piece_refs, (out, pre, act) = refs[:ctx_count], refs[ctx_count:]
        load_pieces(perm_ref, me_ref[0], piece_refs, pre, act, heads, rows)
        head_grads(lengths_ref, act, pre, out, heads, rows, ctx_count, 0)

    scalars = [lengths, block_perm, jnp.stack([me_ctx, me_dp])]
    grad_pre = [
        call(attention, scalars, arrived[part], [bf16(whole, wide)], scratch, part_flops)[0]
        for part in range(parts)
    ]

    def input_terms(perm_ref, me_ref, *refs):
        grads = refs[:parts]
        bands = refs[parts : parts + dp_count]
        outs = refs[parts + dp_count : parts + dp_count + ctx_count]
        band = refs[-1]
        for r in range(dp_count):
            band[pl.ds(pl.multiple_of((me_ref[1] ^ r) * w_rows, w_rows), w_rows), :] = bands[r][...]
        for r in range(ctx_count):
            at = pl.ds(pl.multiple_of(perm_ref[0, me_ref[0] ^ r] * rows, rows), rows)
            total = None
            for part in range(parts):
                term = dot(grads[part][at, :], band[:, part * wide : (part + 1) * wide], BY_COLS)
                total = term if total is None else total + term
            outs[r][...] = total.astype(jnp.bfloat16)

    terms = call(
        input_terms,
        scalars[1:],
        grad_pre + weights,
        [bf16(rows, width)] * ctx_count,
        [pltpu.VMEM((width, columns), jnp.bfloat16)],
        product_flops,
    )
    returned = [terms[0]] + [swap(terms[r], "ctx", r) for r in range(1, ctx_count)]

    def weight_terms(perm_ref, me_ref, *refs):
        grads = refs[:parts]
        token_refs = refs[parts : parts + ctx_count]
        keep, send, held = refs[parts + ctx_count :]
        for r in range(ctx_count):
            at = pl.ds(pl.multiple_of(perm_ref[0, me_ref[0] ^ r] * rows, rows), rows)
            held[at, :] = token_refs[r][...]
        for part in range(parts):
            total = dot(held[...], grads[part][...], BY_ROWS)
            keep[:, part * wide : (part + 1) * wide] = total
        for r in range(0, dp_count, 2):
            at = pl.ds(pl.multiple_of((me_ref[1] ^ r ^ 1) * w_rows, w_rows), w_rows)
            send[r // 2] = keep[at, :].astype(jnp.bfloat16)

    keep, send = call(
        weight_terms,
        scalars[1:],
        grad_pre + tokens,
        [f32(width, columns), bf16(dp_count // 2, w_rows, columns)],
        [pltpu.VMEM((whole, width), jnp.bfloat16)],
        product_flops,
    )
    other = swap(send, "dp", 1)

    def chip_terms(me_ref, keep_ref, other_ref, own, *outs):
        for r in range(0, dp_count, 2):
            at = pl.ds(pl.multiple_of((me_ref[1] ^ r) * w_rows, w_rows), w_rows)
            total = keep_ref[at, :] + other_ref[r // 2].astype(jnp.float32)
            if r == 0:
                own[...] = total
            else:
                outs[r // 2 - 1][...] = total.astype(jnp.bfloat16)

    own, *outgoing = call(
        chip_terms,
        scalars[2:],
        [keep, other],
        [f32(w_rows, columns)] + [bf16(w_rows, columns)] * (dp_count // 2 - 1),
    )
    incoming = [swap(block, "dp", 2 * (i + 1)) for i, block in enumerate(outgoing)]
    total = own
    for block in incoming:
        total = total + block.astype(jnp.float32)
    grad_weight = total * (1.0 / dp_count)
    input_grad = returned[0].astype(jnp.float32)
    for block in returned[1:]:
        input_grad = input_grad + block.astype(jnp.float32)
    return (input_grad.astype(jnp.bfloat16)[None], grad_weight)


def solution(mesh):
    return jax.shard_map(
        body,
        mesh=mesh,
        in_specs=(
            P("dp", "ctx", None),
            P("dp", "ctx", None),
            P("dp", "ctx", None),
            P("dp", "ctx"),
            P("dp", None),
            P("dp", None),
        ),
        out_specs=(P("dp", "ctx", None), P("dp", "ctx")),
        check_vma=False,
    )
```

```python
import jax
import jax.numpy as jnp
from jax import lax
from jax.experimental import pallas as pl
from jax.experimental.pallas import tpu as pltpu
from jax.sharding import PartitionSpec as P

DH = 64
LANES = 128
VMEM_BYTES = 48 * 1024 * 1024
PLAIN = (((1,), (0,)), ((), ()))
BY_ROWS = (((0,), (0,)), ((), ()))
BY_COLS = (((1,), (1,)), ((), ()))


def dot(a, b, dims=PLAIN):
    return lax.dot_general(a, b, dims, preferred_element_type=jnp.float32)


def call(kernel, scalars, arrays, outs, scratch=(), flops=0, place=pltpu.VMEM):
    size = sum(a.size * a.dtype.itemsize for a in arrays) + sum(
        o.size * o.dtype.itemsize for o in outs
    )
    return pl.pallas_call(
        kernel,
        out_shape=list(outs),
        in_specs=[pl.BlockSpec(memory_space=pltpu.SMEM)] * len(scalars)
        + [pl.BlockSpec(memory_space=place)] * len(arrays),
        out_specs=[pl.BlockSpec(memory_space=pltpu.VMEM)] * len(outs),
        scratch_shapes=list(scratch),
        compiler_params=pltpu.CompilerParams(vmem_limit_bytes=VMEM_BYTES),
        cost_estimate=pl.CostEstimate(flops=flops, bytes_accessed=size, transcendentals=0),
    )(*scalars, *arrays)


def bf16(*shape):
    return jax.ShapeDtypeStruct(shape, jnp.bfloat16)


def f32(*shape):
    return jax.ShapeDtypeStruct(shape, jnp.float32)


def after(values, *others):
    return lax.optimization_barrier((values, others))[0]


def swap(array, axis, mask):
    count = lax.axis_size(axis)
    return lax.ppermute(array, axis, [(i, i ^ mask) for i in range(count)])


def row_block(index, rows):
    return pl.ds(pl.multiple_of(index * rows, rows), rows)


def pack(me, pre, grad, count):
    rows = pre.shape[0]
    wide, narrow = pre.shape[1] // count, grad.shape[1] // count
    if wide % LANES or narrow % LANES:
        both = jnp.concatenate(
            [pre.reshape(rows, count, wide), grad.reshape(rows, count, narrow)], axis=2
        ).transpose(1, 0, 2)
        return [lax.dynamic_index_in_dim(both, me ^ r, 0, False) for r in range(count)]

    def kernel(me_ref, pre_ref, grad_ref, *refs):
        outs, sems = refs[:count], refs[count]
        copies = []
        for r in range(count):
            owner = me_ref[0] ^ r
            for i, (ref, at, size) in enumerate(((pre_ref, 0, wide), (grad_ref, wide, narrow))):
                copies.append(
                    pltpu.make_async_copy(
                        ref.at[:, pl.ds(pl.multiple_of(owner * size, LANES), size)],
                        outs[r].at[:, pl.ds(at, size)],
                        sems.at[2 * r + i],
                    )
                )
        for copy in copies:
            copy.start()
        for copy in copies:
            copy.wait()

    return call(
        kernel,
        [me[None]],
        [pre, grad],
        [bf16(rows, wide + narrow)] * count,
        [pltpu.SemaphoreType.DMA((2 * count,))],
        place=pltpu.HBM,
    )


def pair_rows(me, own, other):
    rows = own.shape[0]

    def kernel(me_ref, own_ref, other_ref, out):
        core = me_ref[0] & 1
        out[row_block(core, rows), :] = own_ref[...]
        out[row_block(1 - core, rows), :] = other_ref[...]

    return call(kernel, [me[None]], [own, other], [bf16(2 * rows, own.shape[1])])[0]


def half_columns(me, tokens, count):
    rows, width = tokens.shape
    size = width // count
    if size % LANES:
        blocks = tokens.reshape(rows, count, size)
        return [
            jnp.concatenate(
                [lax.dynamic_index_in_dim(blocks, me ^ r, 1, False) for r in range(i, count, 2)],
                axis=1,
            )
            for i in range(2)
        ]

    def kernel(me_ref, tokens_ref, *outs):
        for r in range(count):
            owner = pl.multiple_of((me_ref[0] ^ r) * size, LANES)
            outs[r % 2][:, r // 2 * size : (r // 2 + 1) * size] = tokens_ref[:, pl.ds(owner, size)]

    return call(kernel, [me[None]], [tokens], [bf16(rows, width // 2)] * 2)


def user_rows(lengths, whole):
    place = lax.broadcasted_iota(jnp.int32, (8, whole), 1)
    first = jnp.zeros((8, whole), jnp.int32)
    length = jnp.zeros((8, whole), jnp.int32)
    start = jnp.int32(0)
    for size in lengths:
        inside = place >= start
        first = jnp.where(inside, start, first)
        length = jnp.where(inside, size, length)
        start = start + size
    return first[:1], lax.rsqrt(length.astype(jnp.float32))[:1]


def attention(perm, lengths, pieces, grad_pre, refs, heads, rows):
    blocks = len(pieces)
    whole = rows * blocks
    wide = heads * 3 * DH
    query_ref, key_ref, value_ref, grad_ref, factor_ref = refs
    for r, piece in enumerate(pieces):
        at = row_block(perm[r], rows)
        z = piece[:, :wide].astype(jnp.float32)
        s = 0.5 + 0.5 * jnp.tanh(0.5 * z)
        active = z * s
        factor_ref[r * rows : (r + 1) * rows, :] = s + active * (1.0 - s)
        active = active.astype(jnp.bfloat16)
        for h in range(heads):
            base = 3 * DH * h
            key = active[:, base + DH : base + 2 * DH]
            query_ref[h, at, :] = active[:, base : base + DH] * jnp.bfloat16(0.0625)
            key_ref[h, at, :] = key
            value_ref[h, at, :] = active[:, base + 2 * DH : base + 3 * DH]
            grad_ref[h, at, :] = piece[:, wide + h * DH : wide + (h + 1) * DH]
    first, scale = user_rows(lengths, whole)
    grad_q = [None] * heads
    for j in range(blocks):
        lo = j * rows
        count = whole - lo
        key_place = lax.broadcasted_iota(jnp.int32, (rows, count), 0)
        query_place = lax.broadcasted_iota(jnp.int32, (rows, count), 1)
        visible = (query_place >= key_place) & (key_place + lo >= first[:, lo:])
        scales = jnp.where(visible, scale[:, lo:], 0.0)
        slot = sum([jnp.where(perm[r] == j, r, 0) for r in range(blocks)])
        done = []
        for h in range(heads):
            query, grad = query_ref[h, lo:, :], grad_ref[h, lo:, :]
            u = dot(key_ref[h, lo : lo + rows, :], query, BY_COLS)
            gw = dot(value_ref[h, lo : lo + rows, :], grad, BY_COLS)
            t = jnp.tanh(u)
            a = scales + scales * t
            weights = (u * a).astype(jnp.bfloat16)
            slope = (gw * a * (1.0 + (u - u * t))).astype(jnp.bfloat16)
            add_q = dot(key_ref[h, lo : lo + rows, :].T, slope)
            total_q = add_q if j == 0 else grad_q[h] + add_q
            grad_q[h] = total_q[:, rows:]
            done += [total_q[:, :rows].T * 0.0625, dot(slope, query), dot(weights, grad)]
        at = row_block(slot, rows)
        grad_pre[at, :] = (jnp.concatenate(done, axis=1) * factor_ref[at, :]).astype(jnp.bfloat16)


def attention_scratch(heads, rows, blocks):
    whole = rows * blocks
    return [pltpu.VMEM((heads, whole, DH), jnp.bfloat16)] * 4 + [
        pltpu.VMEM((whole, heads * 3 * DH), jnp.float32),
    ]


def body(layer_input, projected, grad_output, w_qkv, lengths, block_perm):
    rows, width = layer_input.shape[1:]
    ctx_count, dp_count = lax.axis_size("ctx"), lax.axis_size("dp")
    me_ctx, me_dp = lax.axis_index("ctx"), lax.axis_index("dp")
    whole = rows * ctx_count
    heads = width // DH // ctx_count
    wide = heads * 3 * DH
    users = lengths.shape[1]
    w_rows = w_qkv.shape[0]
    chips = dp_count // 2
    product_flops = 2 * whole * wide * width

    pieces = pack(me_ctx, projected[0], grad_output[0], ctx_count)
    arrived = [pieces[0]] + [None] * (ctx_count - 1)
    for r in range(ctx_count - 1, 0, -1):
        arrived[r] = swap(pieces[r], "ctx", r)

    scalars = jnp.concatenate([me_ctx[None], me_dp[None], lengths[0], block_perm[0]])

    def perm_of(s_ref):
        return [s_ref[2 + users + (s_ref[0] ^ r)] for r in range(ctx_count)]

    pair = pair_rows(me_dp, w_qkv, swap(w_qkv, "dp", 1))
    pair = after(pair, pieces)
    pairs = [pair] + [swap(pair, "dp", 2 * r) for r in range(1, chips)]

    def main(s_ref, *refs):
        attention(
            perm_of(s_ref),
            [s_ref[2 + i] for i in range(users)],
            refs[:ctx_count],
            refs[ctx_count],
            refs[ctx_count + 1 :],
            heads,
            rows,
        )

    grad_pre = call(
        main,
        [scalars],
        arrived,
        [bf16(whole, wide)],
        attention_scratch(heads, rows, ctx_count),
        12 * product_flops,
    )[0]

    kept, sent = half_columns(me_dp, layer_input[0], dp_count)
    sent = after(sent, pieces)
    tokens, mask = {0: jnp.stack([kept, swap(sent, "dp", 1)])}, ctx_count // 2
    tokens[0] = after(tokens[0], arrived[1])
    while mask:
        for r in sorted(tokens):
            tokens[r ^ mask] = swap(after(tokens[r], grad_pre) if r else tokens[r], "ctx", mask)
        mask //= 2
    tokens = [tokens[r] for r in range(ctx_count)]

    grad_pair = swap(grad_pre, "dp", 1)

    def input_terms(s_ref, grad_ref, *refs):
        pair_refs, terms, band = refs[:chips], refs[chips:-1], refs[-1]
        for r in range(chips):
            band[row_block((s_ref[1] >> 1) ^ r, 2 * w_rows), :] = pair_refs[r][...]
        step = min(256, width)
        for at in range(0, width, step):
            product = dot(grad_ref[...], band[at : at + step, :], BY_COLS).astype(jnp.bfloat16)
            for r in range(ctx_count):
                terms[r][:, at : at + step] = product[r * rows : (r + 1) * rows]

    terms = call(
        input_terms,
        [scalars],
        [grad_pre] + pairs,
        [bf16(rows, width)] * ctx_count,
        [pltpu.VMEM((width, wide), jnp.bfloat16)],
        50 * product_flops,
    )
    returned = [terms[0]] + [None] * (ctx_count - 1)
    for r in range(ctx_count - 1, 0, -1):
        returned[r] = swap(terms[r], "ctx", r)

    def weight_terms(own_ref, pair_ref, *refs):
        token_refs = refs[:ctx_count]
        outs, (held, grads) = refs[ctx_count:-2], refs[-2:]
        for r in range(ctx_count):
            for i in range(2):
                at = i * whole + r * rows
                held[at : at + rows, :] = token_refs[r][i]
        grads[:whole, :] = own_ref[...]
        grads[whole:, :] = pair_ref[...]
        product = dot(held[...], grads[...], BY_ROWS)
        for r in range(chips):
            outs[r][...] = product[r * w_rows : (r + 1) * w_rows].astype(outs[r].dtype)

    own, *outgoing = call(
        weight_terms,
        [],
        [grad_pre, grad_pair] + tokens,
        [f32(w_rows, wide)] + [bf16(w_rows, wide)] * (chips - 1),
        [pltpu.VMEM((2 * whole, width // 2), jnp.bfloat16), pltpu.VMEM((2 * whole, wide), jnp.bfloat16)],
        product_flops,
    )
    total = own
    for r in range(1, chips):
        total = total + swap(outgoing[r - 1], "dp", 2 * r).astype(jnp.float32)
    grad_weight = total * (1.0 / dp_count)
    input_grad = returned[0].astype(jnp.float32)
    for block in returned[1:]:
        input_grad = input_grad + block.astype(jnp.float32)
    return (input_grad.astype(jnp.bfloat16)[None], grad_weight)


def solution(mesh):
    return jax.shard_map(
        body,
        mesh=mesh,
        in_specs=(
            P("dp", "ctx", None),
            P("dp", "ctx", None),
            P("dp", "ctx", None),
            P("dp", "ctx"),
            P("dp", None),
            P("dp", None),
        ),
        out_specs=(P("dp", "ctx", None), P("dp", "ctx")),
        check_vma=False,
    )
```

```python
import jax
import jax.numpy as jnp
from jax import lax
from jax.experimental import pallas as pl
from jax.experimental.pallas import tpu as pltpu
from jax.sharding import PartitionSpec as P

DH = 64
LANES = 128
VMEM_BYTES = 48 * 1024 * 1024
PLAIN = (((1,), (0,)), ((), ()))
BY_ROWS = (((0,), (0,)), ((), ()))
BY_COLS = (((1,), (1,)), ((), ()))


def dot(a, b, dims=PLAIN):
    return lax.dot_general(a, b, dims, preferred_element_type=jnp.float32)


def call(kernel, scalars, arrays, outs, scratch=(), flops=0, place=pltpu.VMEM, vmem=VMEM_BYTES):
    size = sum(a.size * a.dtype.itemsize for a in arrays) + sum(
        o.size * o.dtype.itemsize for o in outs
    )
    return pl.pallas_call(
        kernel,
        out_shape=list(outs),
        in_specs=[pl.BlockSpec(memory_space=pltpu.SMEM)] * len(scalars)
        + [pl.BlockSpec(memory_space=place)] * len(arrays),
        out_specs=[pl.BlockSpec(memory_space=pltpu.VMEM)] * len(outs),
        scratch_shapes=list(scratch),
        compiler_params=pltpu.CompilerParams(vmem_limit_bytes=vmem),
        cost_estimate=pl.CostEstimate(flops=flops, bytes_accessed=size, transcendentals=0),
    )(*scalars, *arrays)


def bf16(*shape):
    return jax.ShapeDtypeStruct(shape, jnp.bfloat16)


def f32(*shape):
    return jax.ShapeDtypeStruct(shape, jnp.float32)


def after(values, *others):
    return lax.optimization_barrier((values, others))[0]


def swap(array, axis, mask):
    count = lax.axis_size(axis)
    return lax.ppermute(array, axis, [(i, i ^ mask) for i in range(count)])


def row_block(index, rows):
    return pl.ds(pl.multiple_of(index * rows, rows), rows)


def pack(me, pre, grad, count):
    rows = pre.shape[0]
    wide, narrow = pre.shape[1] // count, grad.shape[1] // count
    if wide % LANES or narrow % LANES:
        both = jnp.concatenate(
            [pre.reshape(rows, count, wide), grad.reshape(rows, count, narrow)], axis=2
        ).transpose(1, 0, 2)
        return [lax.dynamic_index_in_dim(both, me ^ r, 0, False) for r in range(count)]

    def kernel(me_ref, pre_ref, grad_ref, *refs):
        outs, sems = refs[:count], refs[count]
        copies = []
        for r in range(count):
            owner = me_ref[0] ^ r
            for i, (ref, at, size) in enumerate(((pre_ref, 0, wide), (grad_ref, wide, narrow))):
                copies.append(
                    pltpu.make_async_copy(
                        ref.at[:, pl.ds(pl.multiple_of(owner * size, LANES), size)],
                        outs[r].at[:, pl.ds(at, size)],
                        sems.at[2 * r + i],
                    )
                )
        for copy in copies:
            copy.start()
        for copy in copies:
            copy.wait()

    return call(
        kernel,
        [me[None]],
        [pre, grad],
        [bf16(rows, wide + narrow)] * count,
        [pltpu.SemaphoreType.DMA((2 * count,))],
        place=pltpu.HBM,
    )


def pair_rows(me, own, other):
    rows = own.shape[0]

    def kernel(me_ref, own_ref, other_ref, out):
        core = me_ref[0] & 1
        out[row_block(core, rows), :] = own_ref[...]
        out[row_block(1 - core, rows), :] = other_ref[...]

    return call(kernel, [me[None]], [own, other], [bf16(2 * rows, own.shape[1])])[0]


def half_columns(me, own, other, count):
    rows, width = own.shape
    size = width // count
    if size % LANES:
        both = jnp.stack([own, other]).reshape(2, rows, count, size)
        blocks = [lax.dynamic_index_in_dim(both, me ^ r, 2, False) for r in range(0, count, 2)]
        return jnp.concatenate(blocks, axis=2)

    def kernel(me_ref, own_ref, other_ref, out):
        for r in range(0, count, 2):
            owner = pl.ds(pl.multiple_of((me_ref[0] ^ r) * size, LANES), size)
            at = slice(r // 2 * size, (r // 2 + 1) * size)
            out[0, :, at] = own_ref[:, owner]
            out[1, :, at] = other_ref[:, owner]

    return call(kernel, [me[None]], [own, other], [bf16(2, rows, width // 2)])[0]


def user_rows(lengths, whole):
    place = lax.broadcasted_iota(jnp.int32, (8, whole), 1)
    first = jnp.zeros((8, whole), jnp.int32)
    length = jnp.zeros((8, whole), jnp.int32)
    start = jnp.int32(0)
    for size in lengths:
        inside = place >= start
        first = jnp.where(inside, start, first)
        length = jnp.where(inside, size, length)
        start = start + size
    return first[:1], lax.rsqrt(length.astype(jnp.float32))[:1]


def attention(perm, lengths, pieces, grad_pre, refs, heads, rows):
    blocks = len(pieces)
    whole = rows * blocks
    wide = heads * 3 * DH
    query_ref, key_ref, value_ref, grad_ref, factor_ref = refs
    for r, piece in enumerate(pieces):
        at = row_block(perm[r], rows)
        z = piece[:, :wide].astype(jnp.float32)
        s = 0.5 + 0.5 * jnp.tanh(0.5 * z)
        active = z * s
        factor_ref[r * rows : (r + 1) * rows, :] = s + active * (1.0 - s)
        active = active.astype(jnp.bfloat16)
        for h in range(heads):
            base = 3 * DH * h
            key = active[:, base + DH : base + 2 * DH]
            query_ref[h, at, :] = active[:, base : base + DH] * jnp.bfloat16(0.0625)
            key_ref[h, at, :] = key
            value_ref[h, at, :] = active[:, base + 2 * DH : base + 3 * DH]
            grad_ref[h, at, :] = piece[:, wide + h * DH : wide + (h + 1) * DH]
    first, scale = user_rows(lengths, whole)
    step = min(256, whole)
    grad_k, grad_v, grad_q = ([[] for _ in range(heads)] for _ in range(3))
    for lo in range(0, whole, step):
        hi = lo + step
        key_place = lax.broadcasted_iota(jnp.int32, (hi, step), 0)
        query_place = lax.broadcasted_iota(jnp.int32, (hi, step), 1) + lo
        visible = (query_place >= key_place) & (key_place >= first[:, lo:hi])
        scales = jnp.where(visible, scale[:, lo:hi], 0.0)
        for h in range(heads):
            query, grad = query_ref[h, lo:hi, :], grad_ref[h, lo:hi, :]
            key = key_ref[h, :hi, :]
            u = dot(key, query, BY_COLS)
            gw = dot(value_ref[h, :hi, :], grad, BY_COLS)
            t = jnp.tanh(u)
            a = scales + scales * t
            weights = (u * a).astype(jnp.bfloat16)
            slope = (gw * a * (1.0 + (u - u * t))).astype(jnp.bfloat16)
            grad_q[h].append(dot(key.T, slope).T)
            add_k, add_v = dot(slope, query), dot(weights, grad)
            if lo == 0:
                grad_k[h], grad_v[h] = add_k, add_v
            else:
                grad_k[h] = jnp.concatenate([grad_k[h] + add_k[:lo], add_k[lo:]], axis=0)
                grad_v[h] = jnp.concatenate([grad_v[h] + add_v[:lo], add_v[lo:]], axis=0)
    for j in range(blocks):
        slot = sum([jnp.where(perm[r] == j, r, 0) for r in range(blocks)])
        lo, hi = j * rows, (j + 1) * rows
        done = []
        for h in range(heads):
            query = grad_q[h][lo // step]
            done += [query[lo % step : lo % step + rows] * 0.0625, grad_k[h][lo:hi], grad_v[h][lo:hi]]
        at = row_block(slot, rows)
        grad_pre[at, :] = (jnp.concatenate(done, axis=1) * factor_ref[at, :]).astype(jnp.bfloat16)


def attention_scratch(heads, rows, blocks):
    whole = rows * blocks
    return [pltpu.VMEM((heads, whole, DH), jnp.bfloat16)] * 4 + [
        pltpu.VMEM((whole, heads * 3 * DH), jnp.float32),
    ]


def body(layer_input, projected, grad_output, w_qkv, lengths, block_perm):
    rows, width = layer_input.shape[1:]
    ctx_count, dp_count = lax.axis_size("ctx"), lax.axis_size("dp")
    me_ctx, me_dp = lax.axis_index("ctx"), lax.axis_index("dp")
    whole = rows * ctx_count
    heads = width // DH // ctx_count
    wide = heads * 3 * DH
    users = lengths.shape[1]
    w_rows = w_qkv.shape[0]
    chips = dp_count // 2
    product_flops = 2 * whole * wide * width

    pieces = pack(me_ctx, projected[0], grad_output[0], ctx_count)
    arrived = [pieces[0]] + [None] * (ctx_count - 1)
    for r in range(ctx_count - 1, 0, -1):
        arrived[r] = swap(pieces[r], "ctx", r)

    scalars = jnp.concatenate([me_ctx[None], me_dp[None], lengths[0], block_perm[0]])

    def perm_of(s_ref):
        return [s_ref[2 + users + (s_ref[0] ^ r)] for r in range(ctx_count)]

    pair = pair_rows(me_dp, w_qkv, swap(w_qkv, "dp", 1))
    pair = after(pair, pieces)
    pairs = [pair] + [swap(pair, "dp", 2 * r) for r in range(1, chips)]

    def main(s_ref, *refs):
        attention(
            perm_of(s_ref),
            [s_ref[2 + i] for i in range(users)],
            refs[:ctx_count],
            refs[-1],
            refs[ctx_count + 2 : -1],
            heads,
            rows,
        )
        size = whole // 2
        for i in range(2):
            refs[ctx_count + i][...] = refs[-1][i * size : (i + 1) * size, :]

    grad_pre = call(
        main,
        [scalars],
        arrived,
        [bf16(whole // 2, wide)] * 2,
        attention_scratch(heads, rows, ctx_count) + [pltpu.VMEM((whole, wide), jnp.bfloat16)],
        12 * product_flops,
    )
    grad_pre = list(grad_pre)

    def input_terms(s_ref, *refs):
        grad_refs, pair_refs, terms, band = refs[:2], refs[2 : 2 + chips], refs[2 + chips : -1], refs[-1]
        size = ctx_count // 2
        for r in range(chips):
            band[row_block((s_ref[1] >> 1) ^ r, 2 * w_rows), :] = pair_refs[r][...]
        step = min(256, width)
        for at in range(0, width, step):
            for i in range(2):
                product = dot(grad_refs[i][...], band[at : at + step, :], BY_COLS).astype(jnp.bfloat16)
                for r in range(size):
                    terms[i * size + r][:, at : at + step] = product[r * rows : (r + 1) * rows]

    terms = call(
        input_terms,
        [scalars],
        grad_pre + pairs,
        [bf16(rows, width)] * ctx_count,
        [pltpu.VMEM((width, wide), jnp.bfloat16)],
        50 * product_flops,
    )
    returned = [terms[0]] + [None] * (ctx_count - 1)
    for r in range(ctx_count - 1, 0, -1):
        returned[r] = swap(terms[r], "ctx", r)

    tokens = {0: half_columns(me_dp, layer_input[0], swap(layer_input[0], "dp", 1), dp_count)}
    mask = ctx_count // 2
    tokens[0] = tokens[0]
    near = swap(tokens[0], "ctx", 1)
    tokens[0] = after(tokens[0], near, arrived)
    while mask > 1:
        for r in sorted(tokens):
            tokens[r ^ mask] = swap(tokens[r], "ctx", mask)
        mask //= 2
    for r in sorted(tokens):
        tokens[r ^ 1] = swap(tokens[r], "ctx", 1) if r else near
    tokens = [tokens[r] for r in range(ctx_count)]

    grad_pair = [swap(part, "dp", 1) for part in grad_pre]

    def weight_terms(*refs):
        token_refs = refs[2 * 2 : 2 * 2 + ctx_count]
        outs, (held, grads) = refs[2 * 2 + ctx_count : -2], refs[-2:]
        for r in range(ctx_count):
            for i in range(2):
                at = i * whole + r * rows
                held[at : at + rows, :] = token_refs[r][i]
        size = whole // 2
        for i in range(2 * 2):
            grads[i * size : (i + 1) * size, :] = refs[i][...]
        product = dot(held[...], grads[...], BY_ROWS)
        for r in range(chips):
            outs[r][...] = product[r * w_rows : (r + 1) * w_rows].astype(outs[r].dtype)

    own, *outgoing = call(
        weight_terms,
        [],
        grad_pre + grad_pair + tokens,
        [f32(w_rows, wide)] + [bf16(w_rows, wide)] * (chips - 1),
        [pltpu.VMEM((2 * whole, width // 2), jnp.bfloat16), pltpu.VMEM((2 * whole, wide), jnp.bfloat16)],
        product_flops,
    )
    incoming = [swap(block, "dp", 2 * (r + 1)) for r, block in enumerate(outgoing)]

    def sums(own_ref, *refs):
        chip_refs, term_refs = refs[: chips - 1], refs[chips - 1 : chips - 1 + ctx_count]
        weight_out, input_out = refs[-2:]
        total = own_ref[...]
        for ref in chip_refs:
            total = total + ref[...].astype(jnp.float32)
        weight_out[...] = total * (1.0 / dp_count)
        total = term_refs[0][...].astype(jnp.float32)
        for ref in term_refs[1:]:
            total = total + ref[...].astype(jnp.float32)
        input_out[...] = total.astype(jnp.bfloat16)

    grad_weight, input_grad = call(
        sums, [], [own] + incoming + returned, [f32(w_rows, wide), bf16(rows, width)]
    )
    return (input_grad[None], grad_weight)


def solution(mesh):
    return jax.shard_map(
        body,
        mesh=mesh,
        in_specs=(
            P("dp", "ctx", None),
            P("dp", "ctx", None),
            P("dp", "ctx", None),
            P("dp", "ctx"),
            P("dp", None),
            P("dp", None),
        ),
        out_specs=(P("dp", "ctx", None), P("dp", "ctx")),
        check_vma=False,
    )
```

```python
import jax
import jax.numpy as jnp
from jax import lax
from jax.experimental import pallas as pl
from jax.experimental.pallas import tpu as pltpu
from jax.sharding import PartitionSpec as P

DH = 64
LANES = 128
VMEM_BYTES = 48 * 1024 * 1024
PLAIN = (((1,), (0,)), ((), ()))
BY_ROWS = (((0,), (0,)), ((), ()))
BY_COLS = (((1,), (1,)), ((), ()))


def dot(a, b, dims=PLAIN):
    return lax.dot_general(a, b, dims, preferred_element_type=jnp.float32)


def call(kernel, scalars, arrays, outs, scratch=(), flops=0, place=pltpu.VMEM, vmem=VMEM_BYTES):
    size = sum(a.size * a.dtype.itemsize for a in arrays) + sum(
        o.size * o.dtype.itemsize for o in outs
    )
    return pl.pallas_call(
        kernel,
        out_shape=list(outs),
        in_specs=[pl.BlockSpec(memory_space=pltpu.SMEM)] * len(scalars)
        + [pl.BlockSpec(memory_space=place)] * len(arrays),
        out_specs=[pl.BlockSpec(memory_space=pltpu.VMEM)] * len(outs),
        scratch_shapes=list(scratch),
        compiler_params=pltpu.CompilerParams(vmem_limit_bytes=vmem),
        cost_estimate=pl.CostEstimate(flops=flops, bytes_accessed=size, transcendentals=0),
    )(*scalars, *arrays)


def bf16(*shape):
    return jax.ShapeDtypeStruct(shape, jnp.bfloat16)


def f32(*shape):
    return jax.ShapeDtypeStruct(shape, jnp.float32)


def after(values, *others):
    return lax.optimization_barrier((values, others))[0]


def swap(array, axis, mask):
    count = lax.axis_size(axis)
    return lax.ppermute(array, axis, [(i, i ^ mask) for i in range(count)])


def row_block(index, rows):
    return pl.ds(pl.multiple_of(index * rows, rows), rows)


def pack(me, pre, grad, count):
    rows = pre.shape[0]
    wide, narrow = pre.shape[1] // count, grad.shape[1] // count
    if wide % LANES or narrow % LANES:
        both = jnp.concatenate(
            [pre.reshape(rows, count, wide), grad.reshape(rows, count, narrow)], axis=2
        ).transpose(1, 0, 2)
        return [lax.dynamic_index_in_dim(both, me ^ r, 0, False) for r in range(count)]

    def kernel(me_ref, pre_ref, grad_ref, *refs):
        outs, sems = refs[:count], refs[count]
        copies = []
        for r in range(count):
            owner = me_ref[0] ^ r
            for i, (ref, at, size) in enumerate(((pre_ref, 0, wide), (grad_ref, wide, narrow))):
                copies.append(
                    pltpu.make_async_copy(
                        ref.at[:, pl.ds(pl.multiple_of(owner * size, LANES), size)],
                        outs[r].at[:, pl.ds(at, size)],
                        sems.at[2 * r + i],
                    )
                )
        for copy in copies:
            copy.start()
        for copy in copies:
            copy.wait()

    return call(
        kernel,
        [me[None]],
        [pre, grad],
        [bf16(rows, wide + narrow)] * count,
        [pltpu.SemaphoreType.DMA((2 * count,))],
        place=pltpu.HBM,
    )


def pair_rows(me, own, other):
    rows = own.shape[0]

    def kernel(me_ref, own_ref, other_ref, out):
        core = me_ref[0] & 1
        out[row_block(core, rows), :] = own_ref[...]
        out[row_block(1 - core, rows), :] = other_ref[...]

    return call(kernel, [me[None]], [own, other], [bf16(2 * rows, own.shape[1])])[0]


def half_columns(me, own, other, count):
    rows, width = own.shape
    size = width // count
    if size % LANES:
        both = jnp.stack([own, other]).reshape(2, rows, count, size)
        blocks = [lax.dynamic_index_in_dim(both, me ^ r, 2, False) for r in range(0, count, 2)]
        return jnp.concatenate(blocks, axis=2)

    def kernel(me_ref, own_ref, other_ref, out):
        for r in range(0, count, 2):
            owner = pl.ds(pl.multiple_of((me_ref[0] ^ r) * size, LANES), size)
            at = slice(r // 2 * size, (r // 2 + 1) * size)
            out[0, :, at] = own_ref[:, owner]
            out[1, :, at] = other_ref[:, owner]

    return call(kernel, [me[None]], [own, other], [bf16(2, rows, width // 2)])[0]


def user_rows(lengths, whole):
    place = lax.broadcasted_iota(jnp.int32, (8, whole), 1)
    first = jnp.zeros((8, whole), jnp.int32)
    length = jnp.zeros((8, whole), jnp.int32)
    start = jnp.int32(0)
    for size in lengths:
        inside = place >= start
        first = jnp.where(inside, start, first)
        length = jnp.where(inside, size, length)
        start = start + size
    return first[:1], lax.rsqrt(length.astype(jnp.float32))[:1]


def attention(perm, lengths, pieces, grad_pre, refs, heads, rows):
    blocks = len(pieces)
    whole = rows * blocks
    wide = heads * 3 * DH
    query_ref, key_ref, value_ref, grad_ref, factor_ref = refs
    for r, piece in enumerate(pieces):
        at = row_block(perm[r], rows)
        z = piece[:, :wide].astype(jnp.float32)
        s = 0.5 + 0.5 * jnp.tanh(0.5 * z)
        active = z * s
        factor_ref[r * rows : (r + 1) * rows, :] = s + active * (1.0 - s)
        active = active.astype(jnp.bfloat16)
        for h in range(heads):
            base = 3 * DH * h
            key = active[:, base + DH : base + 2 * DH]
            query_ref[h, at, :] = active[:, base : base + DH] * jnp.bfloat16(0.0625)
            key_ref[h, at, :] = key
            value_ref[h, at, :] = active[:, base + 2 * DH : base + 3 * DH]
            grad_ref[h, at, :] = piece[:, wide + h * DH : wide + (h + 1) * DH]
    first, scale = user_rows(lengths, whole)
    step = min(256, whole)
    grad_k, grad_v, grad_q = ([[] for _ in range(heads)] for _ in range(3))
    for lo in range(0, whole, step):
        hi = lo + step
        key_place = lax.broadcasted_iota(jnp.int32, (hi, step), 0)
        query_place = lax.broadcasted_iota(jnp.int32, (hi, step), 1) + lo
        visible = (query_place >= key_place) & (key_place >= first[:, lo:hi])
        scales = jnp.where(visible, scale[:, lo:hi], 0.0)
        for h in range(heads):
            query, grad = query_ref[h, lo:hi, :], grad_ref[h, lo:hi, :]
            key = key_ref[h, :hi, :]
            u = dot(key, query, BY_COLS)
            gw = dot(value_ref[h, :hi, :], grad, BY_COLS)
            t = jnp.tanh(u)
            a = scales + scales * t
            weights = (u * a).astype(jnp.bfloat16)
            slope = (gw * a * (1.0 + (u - u * t))).astype(jnp.bfloat16)
            grad_q[h].append(dot(key.T, slope).T)
            add_k, add_v = dot(slope, query), dot(weights, grad)
            if lo == 0:
                grad_k[h], grad_v[h] = add_k, add_v
            else:
                grad_k[h] = jnp.concatenate([grad_k[h] + add_k[:lo], add_k[lo:]], axis=0)
                grad_v[h] = jnp.concatenate([grad_v[h] + add_v[:lo], add_v[lo:]], axis=0)
    for j in range(blocks):
        slot = sum([jnp.where(perm[r] == j, r, 0) for r in range(blocks)])
        lo, hi = j * rows, (j + 1) * rows
        done = []
        for h in range(heads):
            query = grad_q[h][lo // step]
            done += [query[lo % step : lo % step + rows] * 0.0625, grad_k[h][lo:hi], grad_v[h][lo:hi]]
        at = row_block(slot, rows)
        grad_pre[at, :] = (jnp.concatenate(done, axis=1) * factor_ref[at, :]).astype(jnp.bfloat16)


def attention_scratch(heads, rows, blocks):
    whole = rows * blocks
    return [pltpu.VMEM((heads, whole, DH), jnp.bfloat16)] * 4 + [
        pltpu.VMEM((whole, heads * 3 * DH), jnp.float32),
    ]


def body(layer_input, projected, grad_output, w_qkv, lengths, block_perm):
    rows, width = layer_input.shape[1:]
    ctx_count, dp_count = lax.axis_size("ctx"), lax.axis_size("dp")
    me_ctx, me_dp = lax.axis_index("ctx"), lax.axis_index("dp")
    whole = rows * ctx_count
    heads = width // DH // ctx_count
    wide = heads * 3 * DH
    users = lengths.shape[1]
    w_rows = w_qkv.shape[0]
    chips = dp_count // 2
    product_flops = 2 * whole * wide * width

    pieces = pack(me_ctx, projected[0], grad_output[0], ctx_count)
    arrived = [pieces[0]] + [None] * (ctx_count - 1)
    for r in range(ctx_count - 1, 0, -1):
        arrived[r] = swap(pieces[r], "ctx", r)

    scalars = jnp.concatenate([me_ctx[None], me_dp[None], lengths[0], block_perm[0]])

    def perm_of(s_ref):
        return [s_ref[2 + users + (s_ref[0] ^ r)] for r in range(ctx_count)]

    pair = pair_rows(me_dp, w_qkv, swap(w_qkv, "dp", 1))
    pair = after(pair, pieces)
    pairs = [pair] + [swap(pair, "dp", 2 * r) for r in range(1, chips)]

    def main(s_ref, *refs):
        attention(
            perm_of(s_ref),
            [s_ref[2 + i] for i in range(users)],
            refs[:ctx_count],
            refs[-1],
            refs[ctx_count + 1 : -1],
            heads,
            rows,
        )
        size = whole // 1
        for i in range(1):
            refs[ctx_count + i][...] = refs[-1][i * size : (i + 1) * size, :]

    grad_pre = call(
        main,
        [scalars],
        arrived,
        [bf16(whole // 1, wide)] * 1,
        attention_scratch(heads, rows, ctx_count) + [pltpu.VMEM((whole, wide), jnp.bfloat16)],
        12 * product_flops,
    )
    grad_pre = list(grad_pre)

    def input_terms(s_ref, *refs):
        grad_refs, pair_refs, terms, band = refs[:1], refs[1 : 1 + chips], refs[1 + chips : -1], refs[-1]
        size = ctx_count // 1
        direct = 2 * w_rows % LANES == 0
        step = 2 * w_rows if direct else min(256, width)
        if not direct:
            for r in range(chips):
                band[row_block((s_ref[1] >> 1) ^ r, 2 * w_rows), :] = pair_refs[r][...]
        grads = jnp.concatenate([grad[...] for grad in grad_refs], axis=0)
        for n in range(width // step):
            rhs = pair_refs[n][...] if direct else band[n * step : (n + 1) * step, :]
            at = row_block((s_ref[1] >> 1) ^ n if direct else n, step)
            product = dot(grads, rhs, BY_COLS).astype(jnp.bfloat16)
            for r in range(ctx_count):
                terms[r][:, at] = product[r * rows : (r + 1) * rows]

    terms = call(
        input_terms,
        [scalars],
        grad_pre + pairs,
        [bf16(rows, width)] * ctx_count,
        [pltpu.VMEM((width, wide), jnp.bfloat16)],
        50 * product_flops,
    )
    returned = [terms[0]] + [None] * (ctx_count - 1)
    for r in range(ctx_count - 1, 0, -1):
        returned[r] = swap(terms[r], "ctx", r)

    tokens = {0: half_columns(me_dp, layer_input[0], swap(layer_input[0], "dp", 1), dp_count)}
    mask = ctx_count // 2
    tokens[0] = tokens[0]
    near = swap(tokens[0], "ctx", 1)
    tokens[0] = after(tokens[0], near, arrived[1], arrived[2])
    while mask > 1:
        for r in sorted(tokens):
            tokens[r ^ mask] = swap(tokens[r], "ctx", mask)
        mask //= 2
    for r in sorted(tokens):
        tokens[r ^ 1] = swap(tokens[r], "ctx", 1) if r else near
    tokens = [tokens[r] for r in range(ctx_count)]

    grad_pair = [swap(part, "dp", 1) for part in grad_pre]

    def weight_terms(*refs):
        token_refs = refs[2 * 1 : 2 * 1 + ctx_count]
        outs, (held, grads) = refs[2 * 1 + ctx_count : -2], refs[-2:]
        for r in range(ctx_count):
            for i in range(2):
                at = i * whole + r * rows
                held[at : at + rows, :] = token_refs[r][i]
        size = whole // 1
        for i in range(2 * 1):
            grads[i * size : (i + 1) * size, :] = refs[i][...]
        product = dot(held[...], grads[...], BY_ROWS)
        for r in range(chips):
            outs[r][...] = product[r * w_rows : (r + 1) * w_rows].astype(outs[r].dtype)

    own, *outgoing = call(
        weight_terms,
        [],
        grad_pre + grad_pair + tokens,
        [f32(w_rows, wide)] + [bf16(w_rows, wide)] * (chips - 1),
        [pltpu.VMEM((2 * whole, width // 2), jnp.bfloat16), pltpu.VMEM((2 * whole, wide), jnp.bfloat16)],
        product_flops,
    )
    incoming = [swap(block, "dp", 2 * (r + 1)) for r, block in enumerate(outgoing)]

    def sums(own_ref, *refs):
        chip_refs, term_refs = refs[: chips - 1], refs[chips - 1 : chips - 1 + ctx_count]
        weight_out, input_out = refs[-2:]
        total = own_ref[...]
        for ref in chip_refs:
            total = total + ref[...].astype(jnp.float32)
        weight_out[...] = total * (1.0 / dp_count)
        total = term_refs[0][...].astype(jnp.float32)
        for ref in term_refs[1:]:
            total = total + ref[...].astype(jnp.float32)
        input_out[...] = total.astype(jnp.bfloat16)

    grad_weight, input_grad = call(
        sums, [], [own] + incoming + returned, [f32(w_rows, wide), bf16(rows, width)]
    )
    return (input_grad[None], grad_weight)


def solution(mesh):
    return jax.shard_map(
        body,
        mesh=mesh,
        in_specs=(
            P("dp", "ctx", None),
            P("dp", "ctx", None),
            P("dp", "ctx", None),
            P("dp", "ctx"),
            P("dp", None),
            P("dp", None),
        ),
        out_specs=(P("dp", "ctx", None), P("dp", "ctx")),
        check_vma=False,
    )
```

```python
import jax
import jax.numpy as jnp
from jax import lax
from jax.experimental import pallas as pl
from jax.experimental.pallas import tpu as pltpu
from jax.sharding import PartitionSpec as P

DH = 64
LANES = 128
VMEM_BYTES = 48 * 1024 * 1024
PLAIN = (((1,), (0,)), ((), ()))
BY_ROWS = (((0,), (0,)), ((), ()))
BY_COLS = (((1,), (1,)), ((), ()))


def dot(a, b, dims=PLAIN):
    return lax.dot_general(a, b, dims, preferred_element_type=jnp.float32)


def call(kernel, scalars, arrays, outs, scratch=(), flops=0, place=pltpu.VMEM, vmem=VMEM_BYTES):
    size = sum(a.size * a.dtype.itemsize for a in arrays) + sum(
        o.size * o.dtype.itemsize for o in outs
    )
    return pl.pallas_call(
        kernel,
        out_shape=list(outs),
        in_specs=[pl.BlockSpec(memory_space=pltpu.SMEM)] * len(scalars)
        + [pl.BlockSpec(memory_space=place)] * len(arrays),
        out_specs=[pl.BlockSpec(memory_space=pltpu.VMEM)] * len(outs),
        scratch_shapes=list(scratch),
        compiler_params=pltpu.CompilerParams(vmem_limit_bytes=vmem),
        cost_estimate=pl.CostEstimate(flops=flops, bytes_accessed=size, transcendentals=0),
    )(*scalars, *arrays)


def bf16(*shape):
    return jax.ShapeDtypeStruct(shape, jnp.bfloat16)


def f32(*shape):
    return jax.ShapeDtypeStruct(shape, jnp.float32)


def after(values, *others):
    return lax.optimization_barrier((values, others))[0]


def swap(array, axis, mask):
    count = lax.axis_size(axis)
    return lax.ppermute(array, axis, [(i, i ^ mask) for i in range(count)])


def row_block(index, rows):
    return pl.ds(pl.multiple_of(index * rows, rows), rows)


def pack(me, pre, grad, count):
    rows = pre.shape[0]
    wide, narrow = pre.shape[1] // count, grad.shape[1] // count
    if wide % LANES or narrow % LANES:
        both = jnp.concatenate(
            [pre.reshape(rows, count, wide), grad.reshape(rows, count, narrow)], axis=2
        ).transpose(1, 0, 2)
        return [lax.dynamic_index_in_dim(both, me ^ r, 0, False) for r in range(count)]

    def kernel(me_ref, pre_ref, grad_ref, *refs):
        outs, sems = refs[:count], refs[count]
        copies = []
        for r in range(count):
            owner = me_ref[0] ^ r
            for i, (ref, at, size) in enumerate(((pre_ref, 0, wide), (grad_ref, wide, narrow))):
                copies.append(
                    pltpu.make_async_copy(
                        ref.at[:, pl.ds(pl.multiple_of(owner * size, LANES), size)],
                        outs[r].at[:, pl.ds(at, size)],
                        sems.at[2 * r + i],
                    )
                )
        for copy in copies:
            copy.start()
        for copy in copies:
            copy.wait()

    return call(
        kernel,
        [me[None]],
        [pre, grad],
        [bf16(rows, wide + narrow)] * count,
        [pltpu.SemaphoreType.DMA((2 * count,))],
        place=pltpu.HBM,
    )


def pair_rows(me, own, other):
    rows = own.shape[0]

    def kernel(me_ref, own_ref, other_ref, out):
        core = me_ref[0] & 1
        out[row_block(core, rows), :] = own_ref[...]
        out[row_block(1 - core, rows), :] = other_ref[...]

    return call(kernel, [me[None]], [own, other], [bf16(2 * rows, own.shape[1])])[0]


def half_columns(me, own, other, count):
    rows, width = own.shape
    size = width // count
    if size % LANES:
        both = jnp.stack([own, other]).reshape(2, rows, count, size)
        blocks = [lax.dynamic_index_in_dim(both, me ^ r, 2, False) for r in range(0, count, 2)]
        return jnp.concatenate(blocks, axis=2)

    def kernel(me_ref, own_ref, other_ref, out):
        for r in range(0, count, 2):
            owner = pl.ds(pl.multiple_of((me_ref[0] ^ r) * size, LANES), size)
            at = slice(r // 2 * size, (r // 2 + 1) * size)
            out[0, :, at] = own_ref[:, owner]
            out[1, :, at] = other_ref[:, owner]

    return call(kernel, [me[None]], [own, other], [bf16(2, rows, width // 2)])[0]


def user_rows(lengths, whole):
    place = lax.broadcasted_iota(jnp.int32, (8, whole), 1)
    first = jnp.zeros((8, whole), jnp.int32)
    length = jnp.zeros((8, whole), jnp.int32)
    start = jnp.int32(0)
    for size in lengths:
        inside = place >= start
        first = jnp.where(inside, start, first)
        length = jnp.where(inside, size, length)
        start = start + size
    return first[:1], lax.rsqrt(length.astype(jnp.float32))[:1]


def attention(perm, lengths, pieces, grad_pre, refs, heads, rows):
    blocks = len(pieces)
    whole = rows * blocks
    wide = heads * 3 * DH
    query_ref, key_ref, value_ref, grad_ref, factor_ref = refs
    for r, piece in enumerate(pieces):
        at = row_block(perm[r], rows)
        z = piece[:, :wide].astype(jnp.float32)
        s = 0.5 + 0.5 * jnp.tanh(0.5 * z)
        active = z * s
        factor_ref[r * rows : (r + 1) * rows, :] = s + active * (1.0 - s)
        active = active.astype(jnp.bfloat16)
        for h in range(heads):
            base = 3 * DH * h
            key = active[:, base + DH : base + 2 * DH]
            query_ref[h, at, :] = active[:, base : base + DH] * jnp.bfloat16(0.0625)
            key_ref[h, at, :] = key
            value_ref[h, at, :] = active[:, base + 2 * DH : base + 3 * DH]
            grad_ref[h, at, :] = piece[:, wide + h * DH : wide + (h + 1) * DH]
    first, scale = user_rows(lengths, whole)
    step = min(256, whole)
    grad_k, grad_v, grad_q = ([[] for _ in range(heads)] for _ in range(3))
    for lo in range(0, whole, step):
        hi = lo + step
        key_place = lax.broadcasted_iota(jnp.int32, (hi, step), 0)
        query_place = lax.broadcasted_iota(jnp.int32, (hi, step), 1) + lo
        visible = (query_place >= key_place) & (key_place >= first[:, lo:hi])
        scales = jnp.where(visible, scale[:, lo:hi], 0.0)
        for h in range(heads):
            query, grad = query_ref[h, lo:hi, :], grad_ref[h, lo:hi, :]
            key = key_ref[h, :hi, :]
            u = dot(key, query, BY_COLS)
            gw = dot(value_ref[h, :hi, :], grad, BY_COLS)
            t = jnp.tanh(u)
            a = scales + scales * t
            weights = (u * a).astype(jnp.bfloat16)
            slope = (gw * a * (1.0 + (u - u * t))).astype(jnp.bfloat16)
            grad_q[h].append(dot(key.T, slope).T)
            add_k, add_v = dot(slope, query), dot(weights, grad)
            if lo == 0:
                grad_k[h], grad_v[h] = add_k, add_v
            else:
                grad_k[h] = jnp.concatenate([grad_k[h] + add_k[:lo], add_k[lo:]], axis=0)
                grad_v[h] = jnp.concatenate([grad_v[h] + add_v[:lo], add_v[lo:]], axis=0)
    for j in range(blocks):
        slot = sum([jnp.where(perm[r] == j, r, 0) for r in range(blocks)])
        lo, hi = j * rows, (j + 1) * rows
        done = []
        for h in range(heads):
            query = grad_q[h][lo // step]
            done += [query[lo % step : lo % step + rows] * 0.0625, grad_k[h][lo:hi], grad_v[h][lo:hi]]
        at = row_block(slot, rows)
        grad_pre[at, :] = (jnp.concatenate(done, axis=1) * factor_ref[at, :]).astype(jnp.bfloat16)


def attention_scratch(heads, rows, blocks):
    whole = rows * blocks
    return [pltpu.VMEM((heads, whole, DH), jnp.bfloat16)] * 4 + [
        pltpu.VMEM((whole, heads * 3 * DH), jnp.float32),
    ]


def body(layer_input, projected, grad_output, w_qkv, lengths, block_perm):
    rows, width = layer_input.shape[1:]
    ctx_count, dp_count = lax.axis_size("ctx"), lax.axis_size("dp")
    me_ctx, me_dp = lax.axis_index("ctx"), lax.axis_index("dp")
    whole = rows * ctx_count
    heads = width // DH // ctx_count
    wide = heads * 3 * DH
    users = lengths.shape[1]
    w_rows = w_qkv.shape[0]
    chips = dp_count // 2
    product_flops = 2 * whole * wide * width

    pieces = pack(me_ctx, projected[0], grad_output[0], ctx_count)
    arrived = [pieces[0]] + [None] * (ctx_count - 1)
    for r in range(ctx_count - 1, 0, -1):
        arrived[r] = swap(pieces[r], "ctx", r)

    scalars = jnp.concatenate([me_ctx[None], me_dp[None], lengths[0], block_perm[0]])

    def perm_of(s_ref):
        return [s_ref[2 + users + (s_ref[0] ^ r)] for r in range(ctx_count)]

    pair = pair_rows(me_dp, w_qkv, swap(w_qkv, "dp", 1))
    pair = after(pair, pieces)
    pairs = [pair] + [swap(pair, "dp", 2 * r) for r in range(1, chips)]

    def main(s_ref, *refs):
        attention(
            perm_of(s_ref),
            [s_ref[2 + i] for i in range(users)],
            refs[:ctx_count],
            refs[-1],
            refs[ctx_count + 1 : -1],
            heads,
            rows,
        )
        size = whole // 1
        for i in range(1):
            refs[ctx_count + i][...] = refs[-1][i * size : (i + 1) * size, :]

    grad_pre = call(
        main,
        [scalars],
        arrived,
        [bf16(whole // 1, wide)] * 1,
        attention_scratch(heads, rows, ctx_count) + [pltpu.VMEM((whole, wide), jnp.bfloat16)],
        12 * product_flops,
    )
    grad_pre = list(grad_pre)

    def input_terms(s_ref, *refs):
        grad_refs, pair_refs, terms, band = refs[:1], refs[1 : 1 + chips], refs[1 + chips : -1], refs[-1]
        size = ctx_count // 1
        direct = 2 * w_rows % LANES == 0
        step = 2 * w_rows if direct else min(256, width)
        if not direct:
            for r in range(chips):
                band[row_block((s_ref[1] >> 1) ^ r, 2 * w_rows), :] = pair_refs[r][...]
        grads = jnp.concatenate([grad[...] for grad in grad_refs], axis=0)
        for n in range(width // step):
            rhs = pair_refs[n][...] if direct else band[n * step : (n + 1) * step, :]
            at = row_block((s_ref[1] >> 1) ^ n if direct else n, step)
            product = dot(grads, rhs, BY_COLS).astype(jnp.bfloat16)
            for r in range(ctx_count):
                terms[r][:, at] = product[r * rows : (r + 1) * rows]

    terms = call(
        input_terms,
        [scalars],
        grad_pre + pairs,
        [bf16(rows, width)] * ctx_count,
        [pltpu.VMEM((width, wide), jnp.bfloat16)],
        50 * product_flops,
    )
    returned = [terms[0]] + [None] * (ctx_count - 1)
    for r in range(ctx_count - 1, 0, -1):
        returned[r] = swap(terms[r], "ctx", r)

    tokens = {0: half_columns(me_dp, layer_input[0], swap(layer_input[0], "dp", 1), dp_count)}
    mask = ctx_count // 2
    tokens[0] = tokens[0]
    near = swap(after(tokens[0], pair), "ctx", 1)
    tokens[0] = after(tokens[0], near, arrived[1], arrived[2])
    while mask > 1:
        for r in sorted(tokens):
            tokens[r ^ mask] = swap(tokens[r], "ctx", mask)
        mask //= 2
    for r in sorted(tokens):
        tokens[r ^ 1] = swap(tokens[r], "ctx", 1) if r else near
    tokens = [tokens[r] for r in range(ctx_count)]

    grad_pair = [swap(part, "dp", 1) for part in grad_pre]

    def weight_terms(*refs):
        token_refs = refs[2 * 1 : 2 * 1 + ctx_count]
        outs, (held, grads) = refs[2 * 1 + ctx_count : -2], refs[-2:]
        for r in range(ctx_count):
            for i in range(2):
                at = i * whole + r * rows
                held[at : at + rows, :] = token_refs[r][i]
        size = whole // 1
        for i in range(2 * 1):
            grads[i * size : (i + 1) * size, :] = refs[i][...]
        product = dot(held[...], grads[...], BY_ROWS)
        for r in range(chips):
            outs[r][...] = product[r * w_rows : (r + 1) * w_rows].astype(outs[r].dtype)

    own, *outgoing = call(
        weight_terms,
        [],
        grad_pre + grad_pair + tokens,
        [f32(w_rows, wide)] + [bf16(w_rows, wide)] * (chips - 1),
        [pltpu.VMEM((2 * whole, width // 2), jnp.bfloat16), pltpu.VMEM((2 * whole, wide), jnp.bfloat16)],
        product_flops,
    )
    incoming = [swap(block, "dp", 2 * (r + 1)) for r, block in enumerate(outgoing)]

    def sums(own_ref, *refs):
        chip_refs, term_refs = refs[: chips - 1], refs[chips - 1 : chips - 1 + ctx_count]
        weight_out, input_out = refs[-2:]
        total = own_ref[...]
        for ref in chip_refs:
            total = total + ref[...].astype(jnp.float32)
        weight_out[...] = total * (1.0 / dp_count)
        total = term_refs[0][...].astype(jnp.float32)
        for ref in term_refs[1:]:
            total = total + ref[...].astype(jnp.float32)
        input_out[...] = total.astype(jnp.bfloat16)

    grad_weight, input_grad = call(
        sums, [], [own] + incoming + returned, [f32(w_rows, wide), bf16(rows, width)]
    )
    return (input_grad[None], grad_weight)


def solution(mesh):
    return jax.shard_map(
        body,
        mesh=mesh,
        in_specs=(
            P("dp", "ctx", None),
            P("dp", "ctx", None),
            P("dp", "ctx", None),
            P("dp", "ctx"),
            P("dp", None),
            P("dp", None),
        ),
        out_specs=(P("dp", "ctx", None), P("dp", "ctx")),
        check_vma=False,
    )
```
